32 devices in a mesh: groups: 2 (over x), rows: 16 (over z, y, core).
Axes of the slice: x: 2, y: 2, z: 4, core: 2. Of those that a mesh axis runs over, the one named last changes fastest.
Arguments:
- source: float32 [64, 4096], P(None, ('groups', 'rows')), parts along dimension 1, may hold values from -48 to 48
- target: float32 [64, 4096], P(None, ('groups', 'rows')), parts along dimension 1, may hold values from -48 to 48
Outputs:
- source_potential: float32 [4096], P(('groups', 'rows')), parts along dimension 0
- target_potential: float32 [4096], P(('groups', 'rows')), parts along dimension 0
- grad_source: float32 [64, 4096], P(None, ('groups', 'rows')), parts along dimension 1
- grad_target: float32 [64, 4096], P(None, ('groups', 'rows')), parts along dimension 1
The draws below stay inside these ranges and needn't reach their ends.
There are 2 independent parts, one for each index of `groups`. The reference program is written for one: setup_inputs(seed, part) draws one part's arguments, and reference() takes and returns one part's arrays. A program takes and returns all parts, laid end to end along the dimension named above; each array names one. Nothing has to cross between parts.
All inputs are finite; a program needn't handle non-finite values.
Results may differ from the reference program's by a relative error of at most 0.0003.
Values sent between devices are 32-bit elements; how exact they have to be, the bound alone decides.
A program may use at most 64 MiB of HBM per device.

```python
import math
import jax
import jax.numpy as jnp
from jax import lax

D = 64
ITERS = 4
NPTS = 2048


def point_cloud(key):
    base = jnp.clip(jax.random.normal(key, (D, NPTS), jnp.float32), -6.0, 6.0)
    return base


def draw_source(key, part):
    return point_cloud(jax.random.fold_in(key, 11))


def draw_target(key, part):
    return point_cloud(jax.random.fold_in(key, 23))


def setup_inputs(seed: int = 0, part: int = 0) -> dict:
    key_of = jax.random.split(jax.random.key(seed), 3)
    own_keys = jax.random.split(jax.random.fold_in(key_of[2], part), 3)
    source = draw_source(jax.random.fold_in(jax.random.fold_in(key_of[2], part), 71), part)
    target = draw_target(jax.random.fold_in(jax.random.fold_in(key_of[2], part), 71), part)
    return dict(source=source, target=target)


softness = 0.2


def scores_of(left, right, potential):
    cross = lax.dot_general(left, right, (((0,), (0,)), ((), ())), precision=lax.Precision.HIGHEST, preferred_element_type=jnp.float32)
    left_sq = jnp.sum(left * left, axis=0)
    right_sq = jnp.sum(right * right, axis=0)
    cost = (left_sq[:, None] + right_sq[None, :] - 2.0 * cross) / left.shape[0]
    return (potential[None, :] - cost) / softness


def soft_pass(left, right, potential, with_mean):
    features, npoints = left.shape
    span = math.gcd(npoints, 512)
    blocks = npoints // span
    left_blocks = jnp.moveaxis(left.reshape(features, blocks, span), 1, 0)

    def block_stats(left_block):
        scores = scores_of(left_block, right, potential)
        maxima = jnp.max(scores, axis=1)
        weights = jnp.exp(scores - maxima[:, None])
        totals = jnp.sum(weights, axis=1)
        log_total = maxima + jnp.log(totals)
        if with_mean:
            weighted = lax.dot_general(right, weights, (((1,), (1,)), ((), ())), precision=lax.Precision.HIGHEST, preferred_element_type=jnp.float32)
            return log_total, weighted / totals[None, :]
        return log_total

    results = lax.map(block_stats, left_blocks)
    if with_mean:
        log_total = results[0].reshape(npoints)
        means = jnp.moveaxis(results[1], 0, 1).reshape(features, npoints)
        return log_total, means
    return results.reshape(npoints)


def reference(source, target):
    log_count = math.log(NPTS)
    g_pot = jnp.zeros((NPTS,), jnp.float32)
    f_pot = jnp.zeros((NPTS,), jnp.float32)
    for step_index in range(ITERS):
        f_pot = -softness * (log_count + soft_pass(source, target, g_pot, False))
        g_pot = -softness * (log_count + soft_pass(target, source, f_pot, False))
    row_lse, row_mean = soft_pass(source, target, g_pot, True)
    row_mass = jnp.exp(f_pot / softness + row_lse + log_count)
    grad_source = row_mass[None, :] * (source - row_mean)
    col_lse, col_mean = soft_pass(target, source, f_pot, True)
    grad_target = target - col_mean
    return f_pot, g_pot, grad_source, grad_target
```

```python
import functools
import math

import jax
import jax.numpy as jnp
from jax import lax
from jax.experimental import pallas as pl
from jax.experimental.pallas import tpu as pltpu
from jax.sharding import PartitionSpec as P

ITERS = 4
SOFTNESS = 0.2
LN2 = math.log(2.0)
HIGHEST = lax.Precision.HIGHEST
MESH = pl.DeviceIdType.MESH


def split(rows):
    src = 1
    while (src * 2) ** 2 <= rows and rows % (src * 2) == 0:
        src *= 2
    return src, rows // src


def lse2(stack):
    top = jnp.max(stack, axis=0)
    return top + jnp.log2(jnp.sum(jnp.exp2(stack - top[None]), axis=0))


def kernel(
    src,
    tgt,
    s_hbm,
    t_hbm,
    f_ref,
    g_ref,
    gs_ref,
    gt_ref,
    s_all,
    t_all,
    cross,
    weights,
    f_out,
    f_in,
    g_out,
    g_in,
    u_out,
    u_in,
    w_out,
    w_in,
    local_sem,
    point_send,
    point_recv,
    f_send,
    f_recv,
    g_send,
    g_recv,
    u_send,
    u_recv,
    w_send,
    w_recv,
):
    feats, n = s_hbm.shape
    rank = lax.axis_index("rows")
    b = lax.rem(rank, src)
    a = lax.div(rank, src)
    log_count = math.log2(n * src * tgt)
    scale = 1.0 / (feats * SOFTNESS * LN2)

    def src_peer(k):
        return {"rows": a * src + lax.rem(b + k, src)}

    def tgt_peer(k):
        return {"rows": lax.rem(a + k, tgt) * src + b}

    local_s = pltpu.make_async_copy(s_hbm, s_all.at[0], local_sem.at[0])
    local_t = pltpu.make_async_copy(t_hbm, t_all.at[0], local_sem.at[1])
    local_s.start()
    local_t.start()

    barrier = pltpu.get_barrier_semaphore()
    for k in range(1, src):
        pl.semaphore_signal(barrier, inc=1, device_id=src_peer(k), device_id_type=MESH)
    for k in range(1, tgt):
        pl.semaphore_signal(barrier, inc=1, device_id=tgt_peer(k), device_id_type=MESH)
    pl.semaphore_wait(barrier, src + tgt - 2)

    pending = []

    def send(source, target, send_sem, recv_sem, peer):
        copy = pltpu.make_async_remote_copy(
            src_ref=source, dst_ref=target, send_sem=send_sem, recv_sem=recv_sem, device_id=peer, device_id_type=MESH
        )
        copy.start()
        pending.append(copy)
        return copy

    t_copies, s_copies = {}, {}
    for k in range(max(src, tgt) - 1, 0, -1):
        if k < tgt:
            t_copies[k] = send(t_hbm, t_all.at[k], point_send.at[1, k], point_recv.at[1, k], tgt_peer(k))
        if k < src:
            s_copies[k] = send(s_hbm, s_all.at[k], point_send.at[0, k], point_recv.at[0, k], src_peer(k))

    eye = lax.broadcasted_iota(jnp.int32, (n, n), 0) == lax.broadcasted_iota(jnp.int32, (n, n), 1)

    def to_row(col):
        return jnp.sum(jnp.where(eye, jnp.broadcast_to(col, (n, n)), 0.0), axis=0, keepdims=True)

    def to_col(row):
        return jnp.sum(jnp.where(eye, jnp.broadcast_to(row, (n, n)), 0.0), axis=1, keepdims=True)

    local_s.wait()
    local_t.wait()
    for k in range(1, src):
        s_copies[k].wait_recv()
    lefts = jnp.concatenate([(s_all[p] * (2.0 * scale)).T for p in range(src)], axis=0)
    g_rows = []
    for q in range(tgt):
        if q:
            t_copies[q].wait_recv()
        t = t_all[q]
        g_rows.append(-scale * jnp.sum(t * t, axis=0, keepdims=True))
        cross[:, q * n : (q + 1) * n] = jnp.dot(lefts, t, precision=HIGHEST, preferred_element_type=jnp.float32)

    def row_weights(p, g_row):
        x = cross[p * n : (p + 1) * n, :] + g_row
        top = jnp.max(x, axis=1, keepdims=True)
        w = jnp.exp2(x - top)
        return top, w, jnp.sum(w, axis=1, keepdims=True)

    f_hat = None
    g_hat = None
    for it in range(ITERS):
        last = it == ITERS - 1
        g_row = jnp.concatenate(g_rows, axis=1)
        for p in range(src):
            top, w, total = row_weights(p, g_row)
            part = to_row(top + jnp.log2(total))
            f_out[it, p] = part
            f_out[it, src + p] = part
            f_in[it, 0, p] = part
        copies = [
            send(f_out.at[it, pl.ds(src - k, src)], f_in.at[it, k], f_send.at[it, k], f_recv.at[it, k], src_peer(k))
            for k in range(1, src)
        ]
        for copy in copies:
            copy.wait_recv()
        f_hat = -(log_count + lse2(f_in[it]))
        cols = [to_col(f_hat[p]) for p in range(src)]
        top = None
        for p in range(src):
            piece = jnp.max(cross[p * n : (p + 1) * n, :] + cols[p], axis=0, keepdims=True)
            top = piece if top is None else jnp.maximum(top, piece)
        total = None
        for p in range(src):
            w = jnp.exp2((cross[p * n : (p + 1) * n, :] + cols[p]) - top)
            if last:
                weights[p * n : (p + 1) * n, :] = w
            piece = jnp.sum(w, axis=0, keepdims=True)
            total = piece if total is None else total + piece
        part = top + jnp.log2(total)
        for q in range(tgt):
            piece = part[:, q * n : (q + 1) * n]
            g_out[it, q] = piece
            g_out[it, tgt + q] = piece
            g_in[it, 0, q] = piece
        copies = [
            send(g_out.at[it, pl.ds(tgt - k, tgt)], g_in.at[it, k], g_send.at[it, k], g_recv.at[it, k], tgt_peer(k))
            for k in range(1, tgt)
        ]
        if last:
            means = jnp.dot(
                jnp.concatenate([s_all[p] for p in range(src)], axis=1),
                weights[...],
                precision=HIGHEST,
                preferred_element_type=jnp.float32,
            ) * (1.0 / total)
            for q in range(tgt):
                u_out[q] = means[:, q * n : (q + 1) * n]
            u_copies = [
                send(u_out.at[q], u_in.at[q], u_send.at[q], u_recv.at[q], tgt_peer(tgt - q)) for q in range(1, tgt)
            ]
        for copy in copies:
            copy.wait_recv()
        g_hat = -(log_count + lse2(g_in[it]))
        g_rows = [g_hat[q] for q in range(tgt)]

    g_row = jnp.concatenate(g_rows, axis=1)
    rights = jnp.concatenate([t_all[q] for q in range(tgt)], axis=1)
    w_copies = []
    for p in list(range(1, src)) + [0]:
        top, w, total = row_weights(p, g_row)
        mean = lax.dot_general(
            rights, w, (((1,), (1,)), ((), ())), precision=HIGHEST, preferred_element_type=jnp.float32
        )
        w_out[p, :feats, :] = mean * to_row(1.0 / total)
        w_out[p, feats:, :] = jnp.broadcast_to(to_row(top + jnp.log2(total)), (8, n))
        if p:
            w_copies.append(send(w_out.at[p], w_in.at[p], w_send.at[p], w_recv.at[p], src_peer(src - p)))

    s = s_all[0]
    t = t_all[0]
    f_ref[...] = (f_hat[0] + scale * jnp.sum(s * s, axis=0, keepdims=True)) * (SOFTNESS * LN2)
    g_ref[...] = (g_hat[0] + scale * jnp.sum(t * t, axis=0, keepdims=True)) * (SOFTNESS * LN2)

    for copy in u_copies:
        copy.wait_recv()
    col_lse = -(g_hat[0] + log_count)
    mean = u_out[0] * jnp.exp2(g_in[ITERS - 1, 0, 0] - col_lse)
    for q in range(1, tgt):
        mean = mean + u_in[q] * jnp.exp2(g_in[ITERS - 1, tgt - q, 0] - col_lse)
    gt_ref[...] = t - mean

    for copy in w_copies:
        copy.wait_recv()
    parts = [w_out[0, feats : feats + 1, :]] + [w_in[p, feats : feats + 1, :] for p in range(1, src)]
    row_lse = lse2(jnp.stack(parts))
    mean = w_out[0, :feats, :] * jnp.exp2(parts[0] - row_lse)
    for p in range(1, src):
        mean = mean + w_in[p, :feats, :] * jnp.exp2(parts[p] - row_lse)
    gs_ref[...] = jnp.exp2(f_hat[0] + row_lse + log_count) * (s - mean)

    for copy in pending:
        copy.wait_send()


def solution(mesh):
    src, tgt = split(mesh.shape["rows"])

    def local(source, target):
        feats, n = source.shape
        f32 = jnp.float32
        dma = pltpu.SemaphoreType.DMA
        row = jax.ShapeDtypeStruct((1, n), f32)
        block = jax.ShapeDtypeStruct((feats, n), f32)
        f, g, gs, gt = pl.pallas_call(
            functools.partial(kernel, src, tgt),
            out_shape=(row, row, block, block),
            in_specs=[pl.BlockSpec(memory_space=pl.ANY)] * 2,
            out_specs=tuple([pl.BlockSpec(memory_space=pltpu.VMEM)] * 4),
            scratch_shapes=[
                pltpu.VMEM((src, feats, n), f32),
                pltpu.VMEM((tgt, feats, n), f32),
                pltpu.VMEM((src * n, tgt * n), f32),
                pltpu.VMEM((src * n, tgt * n), f32),
                pltpu.VMEM((ITERS, 2 * src, 1, n), f32),
                pltpu.VMEM((ITERS, src, src, 1, n), f32),
                pltpu.VMEM((ITERS, 2 * tgt, 1, n), f32),
                pltpu.VMEM((ITERS, tgt, tgt, 1, n), f32),
                pltpu.VMEM((tgt, feats, n), f32),
                pltpu.VMEM((tgt, feats, n), f32),
                pltpu.VMEM((src, feats + 8, n), f32),
                pltpu.VMEM((src, feats + 8, n), f32),
                dma((2,)),
                dma((2, max(src, tgt))),
                dma((2, max(src, tgt))),
                dma((ITERS, src)),
                dma((ITERS, src)),
                dma((ITERS, tgt)),
                dma((ITERS, tgt)),
                dma((tgt,)),
                dma((tgt,)),
                dma((src,)),
                dma((src,)),
            ],
            compiler_params=pltpu.CompilerParams(
                collective_id=0, has_side_effects=True, vmem_limit_bytes=48 * 1024 * 1024
            ),
        )(source, target)
        return f.reshape(n), g.reshape(n), gs, gt

    spec = P(("groups", "rows"))
    wide = P(None, ("groups", "rows"))
    return jax.shard_map(
        local, mesh=mesh, in_specs=(wide, wide), out_specs=(spec, spec, wide, wide), check_vma=False
    )
```

```python
import functools
import math

import jax
import jax.numpy as jnp
from jax import lax
from jax.experimental import pallas as pl
from jax.experimental.pallas import tpu as pltpu
from jax.sharding import PartitionSpec as P

ITERS = 4
SOFTNESS = 0.2
LN2 = math.log(2.0)
HIGHEST = lax.Precision.HIGHEST
MESH = pl.DeviceIdType.MESH


def split(rows):
    src = 2 if rows % 2 == 0 else 1
    return src, rows // src


def lse2(stack):
    top = jnp.max(stack, axis=0)
    return top + jnp.log2(jnp.sum(jnp.exp2(stack - top[None]), axis=0))


def kernel(
    src,
    tgt,
    s_hbm,
    t_hbm,
    f_ref,
    g_ref,
    gs_ref,
    gt_ref,
    s_all,
    t_all,
    cross,
    own_cross,
    f_out,
    f_in,
    f_all,
    g_out,
    g_in,
    w_out,
    w_in,
    local_sem,
    point_send,
    point_recv,
    f_send,
    f_recv,
    g_send,
    g_recv,
    b_send,
    b_recv,
    h_send,
    h_recv,
    w_send,
    w_recv,
):
    feats, n = s_hbm.shape
    rank = lax.axis_index("rows")
    b = lax.rem(rank, src)
    a = lax.div(rank, src)
    log_count = math.log2(n * src * tgt)
    scale = 1.0 / (feats * SOFTNESS * LN2)

    def src_peer(k):
        return {"rows": a * src + lax.rem(b + k, src)}

    def tgt_peer(k):
        return {"rows": lax.rem(a + k, tgt) * src + b}

    local_s = pltpu.make_async_copy(s_hbm, s_all.at[0, 0], local_sem.at[0])
    local_t = pltpu.make_async_copy(t_hbm, t_all.at[0], local_sem.at[1])
    local_s.start()
    local_t.start()

    barrier = pltpu.get_barrier_semaphore()
    for k in range(1, src):
        pl.semaphore_signal(barrier, inc=1, device_id=src_peer(k), device_id_type=MESH)
    for k in range(1, tgt):
        pl.semaphore_signal(barrier, inc=1, device_id=tgt_peer(k), device_id_type=MESH)
    pl.semaphore_wait(barrier, src + tgt - 2)

    pending = []

    def send(source, target, send_sem, recv_sem, peer):
        copy = pltpu.make_async_remote_copy(
            src_ref=source, dst_ref=target, send_sem=send_sem, recv_sem=recv_sem, device_id=peer, device_id_type=MESH
        )
        copy.start()
        pending.append(copy)
        return copy

    t_copies, s_copies = {}, {}
    for k in range(max(src, tgt) - 1, 0, -1):
        if k < tgt:
            t_copies[k] = send(t_hbm, t_all.at[k], point_send.at[1, k], point_recv.at[1, k], tgt_peer(k))
        if k < src:
            s_copies[k] = send(s_hbm, s_all.at[k, 0], point_send.at[0, k], point_recv.at[0, k], src_peer(k))

    eye = lax.broadcasted_iota(jnp.int32, (n, n), 0) == lax.broadcasted_iota(jnp.int32, (n, n), 1)

    def to_row(col):
        return jnp.sum(jnp.where(eye, jnp.broadcast_to(col, (n, n)), 0.0), axis=0, keepdims=True)

    def to_col(row):
        return jnp.sum(jnp.where(eye, jnp.broadcast_to(row, (n, n)), 0.0), axis=1, keepdims=True)

    local_s.wait()
    local_t.wait()
    for k in range(1, src):
        s_copies[k].wait_recv()
    lefts = jnp.concatenate([(s_all[p, 0] * (2.0 * scale)).T for p in range(src)], axis=0)
    g_rows = []
    for q in range(tgt):
        if q:
            t_copies[q].wait_recv()
        t = t_all[q]
        g_rows.append(-scale * jnp.sum(t * t, axis=0, keepdims=True))
        cross[:, q * n : (q + 1) * n] = jnp.dot(lefts, t, precision=HIGHEST, preferred_element_type=jnp.float32)

    def row_weights(p, g_row):
        x = cross[p * n : (p + 1) * n, :] + g_row
        top = jnp.max(x, axis=1, keepdims=True)
        w = jnp.exp2(x - top)
        return top, w, jnp.sum(w, axis=1, keepdims=True)

    own_left = (t_all[0] * (2.0 * scale)).T

    def own_columns(p, k):
        slot = p * tgt + k
        own_cross[:, slot * n : (slot + 1) * n] = jnp.dot(
            own_left, s_all[p, k], precision=HIGHEST, preferred_element_type=jnp.float32
        )

    batches = [list(range(1, tgt))[i :: ITERS - 1] for i in range(ITERS - 1)]
    arriving, handed = {}, []
    f_hat = None
    g_hat = None
    for it in range(ITERS):
        last = it == ITERS - 1
        if it:
            for k in batches[it - 1]:
                arriving[k].wait_recv()
                for p in range(1, src):
                    handed.append(
                        (p, k, send(s_all.at[0, k], s_all.at[p, k], h_send.at[p, k], h_recv.at[p, k], src_peer(p)))
                    )
        if not last:
            for k in batches[it]:
                arriving[k] = send(s_hbm, s_all.at[0, k], b_send.at[k], b_recv.at[k], tgt_peer(k))
        g_row = jnp.concatenate(g_rows, axis=1)
        copies = []
        for p in range(src):
            top, w, total = row_weights(p, g_row)
            part = to_row(top + jnp.log2(total))
            f_out[it, p] = part
            f_in[it, p, 0] = part
            for k in range(1, src):
                to = (p + k) % src
                copies.append(
                    (to, send(f_out.at[it, p], f_in.at[it, to, k], f_send.at[it, to, k], f_recv.at[it, to, k], src_peer(k)))
                )
        f_hat = []
        tops, totals = [], []
        for p in range(src):
            for to, copy in copies:
                if to == p:
                    copy.wait_recv()
            f_hat.append(-(log_count + lse2(f_in[it, p])))
            if last:
                f_all[0, p] = f_hat[p]
            x = cross[p * n : (p + 1) * n, :] + to_col(f_hat[p])
            tops.append(jnp.max(x, axis=0, keepdims=True))
            totals.append(jnp.sum(jnp.exp2(x - tops[p]), axis=0, keepdims=True))
        if last:
            f_copies = [
                send(f_all.at[0], f_all.at[k], b_send.at[tgt + k], b_recv.at[tgt + k], tgt_peer(k))
                for k in range(1, tgt)
            ]
        top = functools.reduce(jnp.maximum, tops)
        total = sum(totals[p] * jnp.exp2(tops[p] - top) for p in range(src))
        part = top + jnp.log2(total)
        for q in range(tgt):
            piece = part[:, q * n : (q + 1) * n]
            g_out[it, q] = piece
            g_out[it, tgt + q] = piece
            g_in[it, 0, q] = piece
        copies = [
            send(g_out.at[it, pl.ds(tgt - k, tgt)], g_in.at[it, k], g_send.at[it, k], g_recv.at[it, k], tgt_peer(k))
            for k in range(1, tgt)
        ]
        if it == 0:
            for p in range(src):
                own_columns(p, 0)
        else:
            for k in batches[it - 1]:
                own_columns(0, k)
        if last:
            for p, k, copy in handed:
                copy.wait_recv()
                own_columns(p, k)
        for copy in copies:
            copy.wait_recv()
        g_hat = -(log_count + lse2(g_in[it]))
        g_rows = [g_hat[q] for q in range(tgt)]

    g_row = jnp.concatenate(g_rows, axis=1)
    rights = jnp.concatenate([t_all[q] for q in range(tgt)], axis=1)
    w_copies = []
    for p in list(range(1, src)) + [0]:
        top, w, total = row_weights(p, g_row)
        mean = lax.dot_general(
            rights, w, (((1,), (1,)), ((), ())), precision=HIGHEST, preferred_element_type=jnp.float32
        )
        w_out[p, :feats, :] = mean * to_row(1.0 / total)
        w_out[p, feats:, :] = jnp.broadcast_to(to_row(top + jnp.log2(total)), (8, n))
        if p:
            w_copies.append(send(w_out.at[p], w_in.at[p], w_send.at[p], w_recv.at[p], src_peer(src - p)))

    s = s_all[0, 0]
    t = t_all[0]
    f_ref[...] = (f_hat[0] + scale * jnp.sum(s * s, axis=0, keepdims=True)) * (SOFTNESS * LN2)
    g_ref[...] = (g_hat[0] + scale * jnp.sum(t * t, axis=0, keepdims=True)) * (SOFTNESS * LN2)

    for copy in f_copies:
        copy.wait_recv()
    slots = [(p, k) for p in range(src) for k in range(tgt)]
    f_row = jnp.concatenate([f_all[k, p] for p, k in slots], axis=1)
    w = jnp.exp2(own_cross[...] + f_row + to_col(g_hat[0] + log_count))
    mean = lax.dot_general(
        jnp.concatenate([s_all[p, k] for p, k in slots], axis=1),
        w,
        (((1,), (1,)), ((), ())),
        precision=HIGHEST,
        preferred_element_type=jnp.float32,
    )
    gt_ref[...] = t - mean

    for copy in w_copies:
        copy.wait_recv()
    parts = [w_out[0, feats : feats + 1, :]] + [w_in[p, feats : feats + 1, :] for p in range(1, src)]
    row_lse = lse2(jnp.stack(parts))
    mean = w_out[0, :feats, :] * jnp.exp2(parts[0] - row_lse)
    for p in range(1, src):
        mean = mean + w_in[p, :feats, :] * jnp.exp2(parts[p] - row_lse)
    gs_ref[...] = jnp.exp2(f_hat[0] + row_lse + log_count) * (s - mean)

    for copy in pending:
        copy.wait_send()


def hand_out(*refs):
    half = len(refs) // 2
    for x, y in zip(refs[:half], refs[half:]):
        y[...] = x[...]


def solution(mesh):
    src, tgt = split(mesh.shape["rows"])

    def local(source, target):
        feats, n = source.shape
        f32 = jnp.float32
        dma = pltpu.SemaphoreType.DMA
        row = jax.ShapeDtypeStruct((1, n), f32)
        block = jax.ShapeDtypeStruct((feats, n), f32)
        f, g, gs, gt = pl.pallas_call(
            functools.partial(kernel, src, tgt),
            out_shape=(row, row, block, block),
            in_specs=[pl.BlockSpec(memory_space=pltpu.HBM)] * 2,
            out_specs=tuple([pl.BlockSpec(memory_space=pltpu.VMEM)] * 4),
            scratch_shapes=[
                pltpu.VMEM((src, tgt, feats, n), f32),
                pltpu.VMEM((tgt, feats, n), f32),
                pltpu.VMEM((src * n, tgt * n), f32),
                pltpu.VMEM((n, src * tgt * n), f32),
                pltpu.VMEM((ITERS, src, 1, n), f32),
                pltpu.VMEM((ITERS, src, src, 1, n), f32),
                pltpu.VMEM((tgt, src, 1, n), f32),
                pltpu.VMEM((ITERS, 2 * tgt, 1, n), f32),
                pltpu.VMEM((ITERS, tgt, tgt, 1, n), f32),
                pltpu.VMEM((src, feats + 8, n), f32),
                pltpu.VMEM((src, feats + 8, n), f32),
                dma((2,)),
                dma((2, max(src, tgt))),
                dma((2, max(src, tgt))),
                dma((ITERS, src, src)),
                dma((ITERS, src, src)),
                dma((ITERS, tgt)),
                dma((ITERS, tgt)),
                dma((2 * tgt,)),
                dma((2 * tgt,)),
                dma((src, tgt)),
                dma((src, tgt)),
                dma((src,)),
                dma((src,)),
            ],
            compiler_params=pltpu.CompilerParams(
                collective_id=0, has_side_effects=True, vmem_limit_bytes=56 * 1024 * 1024
            ),
        )(source, target)
        f, g, gs, gt = pl.pallas_call(hand_out, out_shape=(row, row, block, block))(f, g, gs, gt)
        return f.reshape(n), g.reshape(n), gs, gt

    spec = P(("groups", "rows"))
    wide = P(None, ("groups", "rows"))
    return jax.shard_map(
        local, mesh=mesh, in_specs=(wide, wide), out_specs=(spec, spec, wide, wide), check_vma=False
    )
```

```python
import functools
import math

import jax
import jax.numpy as jnp
from jax import lax
from jax.experimental import pallas as pl
from jax.experimental.pallas import tpu as pltpu
from jax.sharding import PartitionSpec as P

ITERS = 4
SOFTNESS = 0.2
LN2 = math.log(2.0)
HIGHEST = lax.Precision.HIGHEST
MESH = pl.DeviceIdType.MESH


def split(rows):
    src = 2 if rows % 2 == 0 else 1
    return src, rows // src


def lse2(stack):
    top = jnp.max(stack, axis=0)
    return top + jnp.log2(jnp.sum(jnp.exp2(stack - top[None]), axis=0))


def kernel(
    src,
    tgt,
    s_hbm,
    t_hbm,
    f_ref,
    g_ref,
    gs_ref,
    gt_ref,
    s_all,
    t_all,
    cross,
    own_cross,
    f_out,
    f_in,
    f_all,
    g_in,
    w_out,
    w_in,
    local_sem,
    point_send,
    point_recv,
    f_send,
    f_recv,
    g_send,
    g_recv,
    b_send,
    b_recv,
    h_send,
    h_recv,
    w_send,
    w_recv,
):
    feats, n = s_hbm.shape
    rank = lax.axis_index("rows")
    b = lax.rem(rank, src)
    a = lax.div(rank, src)
    log_count = math.log2(n * src * tgt)
    scale = 1.0 / (feats * SOFTNESS * LN2)

    def src_peer(k):
        return {"rows": a * src + lax.rem(b + k, src)}

    pairs = tgt & (tgt - 1) == 0

    def chip(k):
        if not pairs:
            return lax.rem(a + tgt - k, tgt)
        other, bit = a, 1
        while bit <= k:
            if k & bit:
                other = other + bit * (1 - 2 * lax.rem(lax.div(a, bit), 2))
            bit *= 2
        return other

    def tgt_peer(k):
        return {"rows": (chip(k) if pairs else lax.rem(a + k, tgt)) * src + b}

    def chip_slot(c):
        if not pairs:
            return lax.rem(a + tgt - c, tgt)
        return chip(c)

    def core(p):
        return lax.rem(b + src - p, src)

    local_s = pltpu.make_async_copy(s_hbm, s_all.at[0, 0], local_sem.at[0])
    local_t = pltpu.make_async_copy(t_hbm, t_all.at[0], local_sem.at[1])
    local_s.start()
    local_t.start()

    barrier = pltpu.get_barrier_semaphore()
    for k in range(1, src):
        pl.semaphore_signal(barrier, inc=1, device_id=src_peer(k), device_id_type=MESH)
    for k in range(1, tgt):
        pl.semaphore_signal(barrier, inc=1, device_id=tgt_peer(k), device_id_type=MESH)
    pl.semaphore_wait(barrier, src + tgt - 2)

    pending = []

    def send(source, target, send_sem, recv_sem, peer):
        copy = pltpu.make_async_remote_copy(
            src_ref=source, dst_ref=target, send_sem=send_sem, recv_sem=recv_sem, device_id=peer, device_id_type=MESH
        )
        copy.start()
        pending.append(copy)
        return copy

    t_copies, s_copies = {}, {}
    far = tgt // 2
    for k in range(1, src):
        s_copies[k] = send(s_hbm, s_all.at[k, 0], point_send.at[0, k], point_recv.at[0, k], src_peer(k))
    for k in list(range(far, tgt)) + list(range(1, far)):
        if k:
            t_copies[k] = send(t_hbm, t_all.at[k], point_send.at[1, k], point_recv.at[1, k], tgt_peer(k))

    eye = lax.broadcasted_iota(jnp.int32, (n, n), 0) == lax.broadcasted_iota(jnp.int32, (n, n), 1)

    def to_row(col):
        return jnp.sum(jnp.where(eye, jnp.broadcast_to(col, (n, n)), 0.0), axis=0, keepdims=True)

    def to_col(row):
        return jnp.sum(jnp.where(eye, jnp.broadcast_to(row, (n, n)), 0.0), axis=1, keepdims=True)

    local_s.wait()
    local_t.wait()
    for k in range(1, src):
        s_copies[k].wait_recv()
    lefts = jnp.concatenate([(s_all[p, 0] * (2.0 * scale)).T for p in range(src)], axis=0)
    rows_of = lax.broadcasted_iota(jnp.int32, (tgt, n), 0)
    g_hat = jnp.zeros((tgt, n), jnp.float32)
    for q in range(tgt):
        if q:
            t_copies[q].wait_recv()
        t = t_all[q]
        g_hat = jnp.where(rows_of == chip(q), -scale * jnp.sum(t * t, axis=0, keepdims=True), g_hat)
        piece = jnp.dot(lefts, t, precision=HIGHEST, preferred_element_type=jnp.float32)
        columns = pl.ds(pl.multiple_of(chip(q) * n, n), n)
        for p in range(src):
            cross[pl.ds(pl.multiple_of(core(p) * n, n), n), columns] = piece[p * n : (p + 1) * n]

    def wide_row(rows):
        return jnp.concatenate([rows[q : q + 1] for q in range(tgt)], axis=1)

    def row_weights(p, g_row):
        x = cross[p * n : (p + 1) * n, :] + g_row
        top = jnp.max(x, axis=1, keepdims=True)
        w = jnp.exp2(x - top)
        return top, w, jnp.sum(w, axis=1, keepdims=True)

    own_left = (t_all[0] * (2.0 * scale)).T

    def own_columns(p, k):
        slot = p * tgt + k
        own_cross[:, slot * n : (slot + 1) * n] = jnp.dot(
            own_left, s_all[p, k], precision=HIGHEST, preferred_element_type=jnp.float32
        )

    batches = [list(range(1, tgt))[i :: ITERS - 1] for i in range(ITERS - 1)]
    arriving, handed = {}, []
    f_hat = None
    for it in range(ITERS):
        last = it == ITERS - 1
        if it:
            for k in batches[it - 1]:
                arriving[k].wait_recv()
                for p in range(1, src):
                    handed.append(
                        (p, k, send(s_all.at[0, k], s_all.at[p, k], h_send.at[p, k], h_recv.at[p, k], src_peer(p)))
                    )
        if not last:
            for k in batches[it]:
                arriving[k] = send(s_hbm, s_all.at[0, k], b_send.at[k], b_recv.at[k], tgt_peer(k))
        g_row = wide_row(g_hat)
        copies = []
        for p in range(src):
            top, w, total = row_weights(p, g_row)
            part = to_row(top + jnp.log2(total))
            f_out[it, p] = part
            f_in[it, p, 0] = part
            for k in range(1, src):
                copies.append(
                    (p, send(f_out.at[it, p], f_in.at[it, p, k], f_send.at[it, p, k], f_recv.at[it, p, k], src_peer(k)))
                )
        f_hat = []
        tops, totals = [], []
        for p in range(src):
            for to, copy in copies:
                if to == p:
                    copy.wait_recv()
            f_hat.append(-(log_count + lse2(f_in[it, p])))
            x = cross[p * n : (p + 1) * n, :] + to_col(f_hat[p])
            tops.append(jnp.max(x, axis=0, keepdims=True))
            totals.append(jnp.sum(jnp.exp2(x - tops[p]), axis=0, keepdims=True))
        if last:
            f_mine = sum(jnp.where(b == p, f_hat[p], 0.0) for p in range(src))
            for p in range(src):
                f_all[0, p] = f_hat[p]
            f_copies = [
                send(f_all.at[0], f_all.at[k], b_send.at[tgt + k], b_recv.at[tgt + k], tgt_peer(k))
                for k in range(1, tgt)
            ]
        top = functools.reduce(jnp.maximum, tops)
        total = sum(totals[p] * jnp.exp2(tops[p] - top) for p in range(src))
        part = top + jnp.log2(total)
        for q in range(tgt):
            g_in[it, 0, q : q + 1] = part[:, q * n : (q + 1) * n]
        copies = [
            send(g_in.at[it, 0], g_in.at[it, k], g_send.at[it, k], g_recv.at[it, k], tgt_peer(k)) for k in range(1, tgt)
        ]
        if it == 0:
            for p in range(src):
                own_columns(p, 0)
        else:
            for k in batches[it - 1]:
                own_columns(0, k)
        if last:
            for p, k, copy in handed:
                copy.wait_recv()
                own_columns(p, k)
        for copy in copies:
            copy.wait_recv()
        g_hat = -(log_count + lse2(g_in[it]))

    g_row = wide_row(g_hat)
    rights = jnp.concatenate([t_all[chip_slot(q)] for q in range(tgt)], axis=1)
    w_copies = []
    for p in list(range(1, src)) + [0]:
        x = cross[pl.ds(pl.multiple_of(core(p) * n, n), n), :] + g_row
        top = jnp.max(x, axis=1, keepdims=True)
        w = jnp.exp2(x - top)
        total = jnp.sum(w, axis=1, keepdims=True)
        mean = lax.dot_general(
            rights, w, (((1,), (1,)), ((), ())), precision=HIGHEST, preferred_element_type=jnp.float32
        )
        w_out[p, :feats, :] = mean * to_row(1.0 / total)
        w_out[p, feats:, :] = jnp.broadcast_to(to_row(top + jnp.log2(total)), (8, n))
        if p:
            w_copies.append(send(w_out.at[p], w_in.at[p], w_send.at[p], w_recv.at[p], src_peer(src - p)))

    s = s_all[0, 0]
    t = t_all[0]
    g_mine = jnp.sum(jnp.where(rows_of == a, g_hat, 0.0), axis=0, keepdims=True)
    f_ref[...] = (f_mine + scale * jnp.sum(s * s, axis=0, keepdims=True)) * (SOFTNESS * LN2)
    g_ref[...] = (g_mine + scale * jnp.sum(t * t, axis=0, keepdims=True)) * (SOFTNESS * LN2)

    for copy in f_copies:
        copy.wait_recv()

    def f_slot(p, k):
        return sum(jnp.where(core(p) == c, f_all[k, c], 0.0) for c in range(src))

    slots = [(p, k) for p in range(src) for k in range(tgt)]
    f_row = jnp.concatenate([f_slot(p, k) for p, k in slots], axis=1)
    w = jnp.exp2(own_cross[...] + f_row + to_col(g_mine + log_count))
    mean = lax.dot_general(
        jnp.concatenate([s_all[p, k] for p, k in slots], axis=1),
        w,
        (((1,), (1,)), ((), ())),
        precision=HIGHEST,
        preferred_element_type=jnp.float32,
    )
    gt_ref[...] = t - mean

    for copy in w_copies:
        copy.wait_recv()
    parts = [w_out[0, feats : feats + 1, :]] + [w_in[p, feats : feats + 1, :] for p in range(1, src)]
    row_lse = lse2(jnp.stack(parts))
    mean = w_out[0, :feats, :] * jnp.exp2(parts[0] - row_lse)
    for p in range(1, src):
        mean = mean + w_in[p, :feats, :] * jnp.exp2(parts[p] - row_lse)
    gs_ref[...] = jnp.exp2(f_mine + row_lse + log_count) * (s - mean)

    for copy in pending:
        copy.wait_send()


def hand_out(*refs):
    half = len(refs) // 2
    for x, y in zip(refs[:half], refs[half:]):
        y[...] = x[...]


def solution(mesh):
    src, tgt = split(mesh.shape["rows"])

    def local(source, target):
        feats, n = source.shape
        f32 = jnp.float32
        dma = pltpu.SemaphoreType.DMA
        row = jax.ShapeDtypeStruct((1, n), f32)
        block = jax.ShapeDtypeStruct((feats, n), f32)
        f, g, gs, gt = pl.pallas_call(
            functools.partial(kernel, src, tgt),
            out_shape=(row, row, block, block),
            in_specs=[pl.BlockSpec(memory_space=pltpu.HBM)] * 2,
            out_specs=tuple([pl.BlockSpec(memory_space=pltpu.VMEM)] * 4),
            scratch_shapes=[
                pltpu.VMEM((src, tgt, feats, n), f32),
                pltpu.VMEM((tgt, feats, n), f32),
                pltpu.VMEM((src * n, tgt * n), f32),
                pltpu.VMEM((n, src * tgt * n), f32),
                pltpu.VMEM((ITERS, src, 1, n), f32),
                pltpu.VMEM((ITERS, src, src, 1, n), f32),
                pltpu.VMEM((tgt, src, 1, n), f32),
                pltpu.VMEM((ITERS, tgt, tgt, n), f32),
                pltpu.VMEM((src, feats + 8, n), f32),
                pltpu.VMEM((src, feats + 8, n), f32),
                dma((2,)),
                dma((2, max(src, tgt))),
                dma((2, max(src, tgt))),
                dma((ITERS, src, src)),
                dma((ITERS, src, src)),
                dma((ITERS, tgt)),
                dma((ITERS, tgt)),
                dma((2 * tgt,)),
                dma((2 * tgt,)),
                dma((src, tgt)),
                dma((src, tgt)),
                dma((src,)),
                dma((src,)),
            ],
            compiler_params=pltpu.CompilerParams(
                collective_id=0, has_side_effects=True, vmem_limit_bytes=56 * 1024 * 1024
            ),
        )(source, target)
        f, g, gs, gt = pl.pallas_call(hand_out, out_shape=(row, row, block, block))(f, g, gs, gt)
        return f.reshape(n), g.reshape(n), gs, gt

    spec = P(("groups", "rows"))
    wide = P(None, ("groups", "rows"))
    return jax.shard_map(
        local, mesh=mesh, in_specs=(wide, wide), out_specs=(spec, spec, wide, wide), check_vma=False
    )
```

```python
import functools
import math

import jax
import jax.numpy as jnp
from jax import lax
from jax.experimental import pallas as pl
from jax.experimental.pallas import tpu as pltpu
from jax.sharding import PartitionSpec as P

ITERS = 4
SOFTNESS = 0.2
LN2 = math.log(2.0)
HIGHEST = lax.Precision.HIGHEST
MESH = pl.DeviceIdType.MESH


def split(rows):
    src = 2 if rows % 2 == 0 else 1
    return src, rows // src


def lse2(stack):
    top = jnp.max(stack, axis=0)
    return top + jnp.log2(jnp.sum(jnp.exp2(stack - top[None]), axis=0))


def kernel(
    src,
    tgt,
    s_hbm,
    t_hbm,
    f_ref,
    g_ref,
    gs_ref,
    gt_ref,
    s_all,
    t_all,
    cross,
    own_cross,
    f_out,
    f_in,
    f_all,
    g_in,
    w_out,
    w_in,
    local_sem,
    point_send,
    point_recv,
    f_send,
    f_recv,
    g_send,
    g_recv,
    b_send,
    b_recv,
    h_send,
    h_recv,
    w_send,
    w_recv,
):
    feats, n = s_hbm.shape
    rank = lax.axis_index("rows")
    b = lax.rem(rank, src)
    a = lax.div(rank, src)
    log_count = math.log2(n * src * tgt)
    scale = 1.0 / (feats * SOFTNESS * LN2)

    def src_peer(k):
        return {"rows": a * src + lax.rem(b + k, src)}

    pairs = tgt & (tgt - 1) == 0

    def chip(k):
        if not pairs:
            return lax.rem(a + tgt - k, tgt)
        other, bit = a, 1
        while bit <= k:
            if k & bit:
                other = other + bit * (1 - 2 * lax.rem(lax.div(a, bit), 2))
            bit *= 2
        return other

    def tgt_peer(k):
        return {"rows": (chip(k) if pairs else lax.rem(a + k, tgt)) * src + b}

    def chip_slot(c):
        if not pairs:
            return lax.rem(a + tgt - c, tgt)
        return chip(c)

    def core(p):
        return lax.rem(b + src - p, src)

    local_s = pltpu.make_async_copy(s_hbm, s_all.at[0, 0], local_sem.at[0])
    local_t = pltpu.make_async_copy(t_hbm, t_all.at[0], local_sem.at[1])
    local_s.start()
    local_t.start()

    barrier = pltpu.get_barrier_semaphore()
    for k in range(1, src):
        pl.semaphore_signal(barrier, inc=1, device_id=src_peer(k), device_id_type=MESH)
    for k in range(1, tgt):
        pl.semaphore_signal(barrier, inc=1, device_id=tgt_peer(k), device_id_type=MESH)
    pl.semaphore_wait(barrier, src + tgt - 2)

    pending = []

    def send(source, target, send_sem, recv_sem, peer):
        copy = pltpu.make_async_remote_copy(
            src_ref=source, dst_ref=target, send_sem=send_sem, recv_sem=recv_sem, device_id=peer, device_id_type=MESH
        )
        copy.start()
        pending.append(copy)
        return copy

    t_copies, s_copies = {}, {}
    far = tgt // 2
    for k in range(1, src):
        s_copies[k] = send(s_hbm, s_all.at[k, 0], point_send.at[0, k], point_recv.at[0, k], src_peer(k))
    for k in list(range(far, tgt)) + list(range(1, far)):
        if k:
            t_copies[k] = send(t_hbm, t_all.at[k], point_send.at[1, k], point_recv.at[1, k], tgt_peer(k))

    eye = lax.broadcasted_iota(jnp.int32, (n, n), 0) == lax.broadcasted_iota(jnp.int32, (n, n), 1)

    def to_row(col):
        return jnp.sum(jnp.where(eye, jnp.broadcast_to(col, (n, n)), 0.0), axis=0, keepdims=True)

    def to_col(row):
        return jnp.sum(jnp.where(eye, jnp.broadcast_to(row, (n, n)), 0.0), axis=1, keepdims=True)

    local_s.wait()
    local_t.wait()
    for k in range(1, src):
        s_copies[k].wait_recv()
    lefts = jnp.concatenate([(s_all[p, 0] * (2.0 * scale)).T for p in range(src)], axis=0)
    rows_of = lax.broadcasted_iota(jnp.int32, (tgt, n), 0)
    g_hat = jnp.zeros((tgt, n), jnp.float32)
    for q in range(tgt):
        if q:
            t_copies[q].wait_recv()
        t = t_all[q]
        g_hat = jnp.where(rows_of == chip(q), -scale * jnp.sum(t * t, axis=0, keepdims=True), g_hat)
        piece = jnp.dot(lefts, t, precision=HIGHEST, preferred_element_type=jnp.float32)
        columns = pl.ds(pl.multiple_of(chip(q) * n, n), n)
        for p in range(src):
            cross[pl.ds(pl.multiple_of(core(p) * n, n), n), columns] = piece[p * n : (p + 1) * n]

    def wide_row(rows):
        return jnp.concatenate([rows[q : q + 1] for q in range(tgt)], axis=1)

    def row_weights(p, g_row):
        x = cross[p * n : (p + 1) * n, :] + g_row
        top = jnp.max(x, axis=1, keepdims=True)
        w = jnp.exp2(x - top)
        return top, w, jnp.sum(w, axis=1, keepdims=True)

    own_left = (t_all[0] * (2.0 * scale)).T

    def own_columns(p, k):
        slot = p * tgt + k
        own_cross[:, slot * n : (slot + 1) * n] = jnp.dot(
            own_left, s_all[p, k], precision=HIGHEST, preferred_element_type=jnp.float32
        )

    batches = [list(range(1, tgt))[i :: ITERS - 1] for i in range(ITERS - 1)]
    arriving, handed = {}, []
    f_hat = None
    for it in range(ITERS):
        last = it == ITERS - 1
        if it:
            for k in batches[it - 1]:
                arriving[k].wait_recv()
                for p in range(1, src):
                    handed.append(
                        (p, k, send(s_all.at[0, k], s_all.at[p, k], h_send.at[p, k], h_recv.at[p, k], src_peer(p)))
                    )
        if not last:
            for k in batches[it]:
                arriving[k] = send(s_hbm, s_all.at[0, k], b_send.at[k], b_recv.at[k], tgt_peer(k))
        g_row = wide_row(g_hat)
        copies = []
        for p in range(src):
            top, w, total = row_weights(p, g_row)
            part = to_row(top + jnp.log2(total))
            f_out[it, p] = part
            f_in[it, p, 0] = part
            for k in range(1, src):
                copies.append(
                    (p, send(f_out.at[it, p], f_in.at[it, p, k], f_send.at[it, p, k], f_recv.at[it, p, k], src_peer(k)))
                )
        f_hat = []
        tops, totals = [], []
        for p in range(src):
            for to, copy in copies:
                if to == p:
                    copy.wait_recv()
            f_hat.append(-(log_count + lse2(f_in[it, p])))
            x = cross[p * n : (p + 1) * n, :] + to_col(f_hat[p])
            tops.append(jnp.max(x, axis=0, keepdims=True))
            totals.append(jnp.sum(jnp.exp2(x - tops[p]), axis=0, keepdims=True))
        if last:
            f_mine = sum(jnp.where(b == p, f_hat[p], 0.0) for p in range(src))
            for p in range(src):
                f_all[0, p] = f_hat[p]
            f_copies = [
                send(f_all.at[0], f_all.at[k], b_send.at[tgt + k], b_recv.at[tgt + k], tgt_peer(k))
                for k in range(1, tgt)
            ]
        top = functools.reduce(jnp.maximum, tops)
        total = sum(totals[p] * jnp.exp2(tops[p] - top) for p in range(src))
        part = top + jnp.log2(total)
        for q in range(tgt):
            g_in[it, 0, q : q + 1] = part[:, q * n : (q + 1) * n]
        copies = [
            send(g_in.at[it, 0], g_in.at[it, k], g_send.at[it, k], g_recv.at[it, k], tgt_peer(k))
            for k in range(tgt - 1, 0, -1)
        ]
        if it == 0:
            for p in range(src):
                own_columns(p, 0)
        else:
            for k in batches[it - 1]:
                own_columns(0, k)
        if last:
            for p, k, copy in handed:
                copy.wait_recv()
                own_columns(p, k)
        for copy in copies:
            copy.wait_recv()
        g_hat = -(log_count + lse2(g_in[it]))

    g_row = wide_row(g_hat)
    rights = jnp.concatenate([t_all[chip_slot(q)] for q in range(tgt)], axis=1)
    w_copies = []
    for p in list(range(1, src)) + [0]:
        x = cross[pl.ds(pl.multiple_of(core(p) * n, n), n), :] + g_row
        top = jnp.max(x, axis=1, keepdims=True)
        w = jnp.exp2(x - top)
        total = jnp.sum(w, axis=1, keepdims=True)
        mean = lax.dot_general(
            rights, w, (((1,), (1,)), ((), ())), precision=HIGHEST, preferred_element_type=jnp.float32
        )
        w_out[p, :feats, :] = mean * to_row(1.0 / total)
        w_out[p, feats:, :] = jnp.broadcast_to(to_row(top + jnp.log2(total)), (8, n))
        if p:
            w_copies.append(send(w_out.at[p], w_in.at[p], w_send.at[p], w_recv.at[p], src_peer(src - p)))

    s = s_all[0, 0]
    t = t_all[0]
    g_mine = jnp.sum(jnp.where(rows_of == a, g_hat, 0.0), axis=0, keepdims=True)
    f_ref[...] = (f_mine + scale * jnp.sum(s * s, axis=0, keepdims=True)) * (SOFTNESS * LN2)
    g_ref[...] = (g_mine + scale * jnp.sum(t * t, axis=0, keepdims=True)) * (SOFTNESS * LN2)

    for copy in f_copies:
        copy.wait_recv()

    def f_slot(p, k):
        return sum(jnp.where(core(p) == c, f_all[k, c], 0.0) for c in range(src))

    slots = [(p, k) for p in range(src) for k in range(tgt)]
    f_row = jnp.concatenate([f_slot(p, k) for p, k in slots], axis=1)
    w = jnp.exp2(own_cross[...] + f_row + to_col(g_mine + log_count))
    mean = lax.dot_general(
        jnp.concatenate([s_all[p, k] for p, k in slots], axis=1),
        w,
        (((1,), (1,)), ((), ())),
        precision=HIGHEST,
        preferred_element_type=jnp.float32,
    )
    gt_ref[...] = t - mean

    for copy in w_copies:
        copy.wait_recv()
    parts = [w_out[0, feats : feats + 1, :]] + [w_in[p, feats : feats + 1, :] for p in range(1, src)]
    row_lse = lse2(jnp.stack(parts))
    mean = w_out[0, :feats, :] * jnp.exp2(parts[0] - row_lse)
    for p in range(1, src):
        mean = mean + w_in[p, :feats, :] * jnp.exp2(parts[p] - row_lse)
    gs_ref[...] = jnp.exp2(f_mine + row_lse + log_count) * (s - mean)

    for copy in pending:
        copy.wait_send()


def hand_out(*refs):
    half = len(refs) // 2
    for x, y in zip(refs[:half], refs[half:]):
        y[...] = x[...]


def solution(mesh):
    src, tgt = split(mesh.shape["rows"])

    def local(source, target):
        feats, n = source.shape
        f32 = jnp.float32
        dma = pltpu.SemaphoreType.DMA
        row = jax.ShapeDtypeStruct((1, n), f32)
        block = jax.ShapeDtypeStruct((feats, n), f32)
        f, g, gs, gt = pl.pallas_call(
            functools.partial(kernel, src, tgt),
            out_shape=(row, row, block, block),
            in_specs=[pl.BlockSpec(memory_space=pltpu.HBM)] * 2,
            out_specs=tuple([pl.BlockSpec(memory_space=pltpu.VMEM)] * 4),
            scratch_shapes=[
                pltpu.VMEM((src, tgt, feats, n), f32),
                pltpu.VMEM((tgt, feats, n), f32),
                pltpu.VMEM((src * n, tgt * n), f32),
                pltpu.VMEM((n, src * tgt * n), f32),
                pltpu.VMEM((ITERS, src, 1, n), f32),
                pltpu.VMEM((ITERS, src, src, 1, n), f32),
                pltpu.VMEM((tgt, src, 1, n), f32),
                pltpu.VMEM((ITERS, tgt, tgt, n), f32),
                pltpu.VMEM((src, feats + 8, n), f32),
                pltpu.VMEM((src, feats + 8, n), f32),
                dma((2,)),
                dma((2, max(src, tgt))),
                dma((2, max(src, tgt))),
                dma((ITERS, src, src)),
                dma((ITERS, src, src)),
                dma((ITERS, tgt)),
                dma((ITERS, tgt)),
                dma((2 * tgt,)),
                dma((2 * tgt,)),
                dma((src, tgt)),
                dma((src, tgt)),
                dma((src,)),
                dma((src,)),
            ],
            compiler_params=pltpu.CompilerParams(
                collective_id=0, has_side_effects=True, vmem_limit_bytes=56 * 1024 * 1024
            ),
        )(source, target)
        f, g, gs, gt = pl.pallas_call(hand_out, out_shape=(row, row, block, block))(f, g, gs, gt)
        return f.reshape(n), g.reshape(n), gs, gt

    spec = P(("groups", "rows"))
    wide = P(None, ("groups", "rows"))
    return jax.shard_map(
        local, mesh=mesh, in_specs=(wide, wide), out_specs=(spec, spec, wide, wide), check_vma=False
    )
```
